32 devices in a mesh: gx: 4 (over z), gy: 2 (over y), gz: 4 (over x, core).
Axes of the slice: x: 2, y: 2, z: 4, core: 2. Of those that a mesh axis runs over, the one named last changes fastest.
Arguments:
- composition: float32 [12, 8, 16, 512], P(None, 'gx', 'gy', 'gz'), may hold values from -3 to 3
- cotangent: float32 [12, 8, 16, 512], P(None, 'gx', 'gy', 'gz'), may hold values from -4 to 4
- weight_one: bfloat16 [64, 12], replicated, may hold values from -1.75 to 1.75
- bias_one: float32 [64], replicated, may hold values from -0.5 to 0.5
- weight_two: bfloat16 [64, 64], replicated, may hold values from -0.75 to 0.75
- bias_two: float32 [64], replicated, may hold values from -0.5 to 0.5
- weight_three: bfloat16 [144, 64], replicated, may hold values from -0.75 to 0.75
- bias_three: float32 [144], replicated, may hold values from -1 to 1
Outputs:
- grad_composition: float32 [12, 8, 16, 512], P(None, 'gx', 'gy', 'gz')
- grad_weight_one: float32 [64, 12], replicated
- grad_bias_one: float32 [64], replicated
- grad_weight_two: float32 [64, 64], replicated
- grad_bias_two: float32 [64], replicated
- grad_weight_three: float32 [144, 64], replicated
- grad_bias_three: float32 [144], replicated
The draws below stay inside these ranges and needn't reach their ends.
All inputs are finite; a program needn't handle non-finite values.
Results may differ from the reference program's by a relative error of at most 0.0077.
Values sent between devices are 32-bit elements; how exact they have to be, the bound alone decides.
A program may use at most 128 MiB of HBM per device.

```python
import math
import jax
import jax.numpy as jnp
from jax import lax

NC = 12
H1 = 64
H2 = 64
MM = 144
NX = 8
NY = 16
NZ = 512


def block_scale(stream_key, extent, pieces, least, high):
    loudness, own = 1.0, jax.random.fold_in(stream_key, 6)
    for axis_at, shards_of in pieces:
        heights = jnp.exp(jax.random.uniform(jax.random.fold_in(own, axis_at), (shards_of,), jnp.float32, least / len(pieces), high / len(pieces)))
        loudness = loudness * jnp.repeat(heights, extent[axis_at] // shards_of).reshape([-1 if axis == axis_at else 1 for axis in range(len(extent))])
    return loudness


def normal_values(stream_key, dims, width, reach, split=(), kind=jnp.bfloat16):
    entries = width * jax.random.normal(stream_key, dims, jnp.float32)
    if split:
        entries = entries * block_scale(stream_key, dims, split, -0.22, 0.18)
    return jnp.clip(entries, -reach, reach).astype(kind)


def setup_inputs(seed: int = 0) -> dict:
    streams_of = jax.random.split(jax.random.key(seed), 9)
    composition = normal_values(streams_of[0], (NC, NX, NY, NZ), 1.0, 3.0, ((1, 4), (2, 2), (3, 4)), jnp.float32)
    cotangent = normal_values(streams_of[1], (NC, NX, NY, NZ), 1.0, 4.0, ((1, 4), (2, 2), (3, 4)), jnp.float32)
    weight_one = normal_values(streams_of[2], (H1, NC), NC ** -0.5, 1.75)
    bias_one = jnp.clip(jax.random.uniform(streams_of[3], (H1,), jnp.float32, -0.5, 0.5), -0.5, 0.5)
    weight_two = normal_values(streams_of[4], (H2, H1), H1 ** -0.5, 0.75)
    bias_two = jnp.clip(jax.random.uniform(streams_of[5], (H2,), jnp.float32, -0.5, 0.5), -0.5, 0.5)
    weight_three = normal_values(streams_of[6], (MM, H2), H2 ** -0.5, 0.75)
    bias_three = jnp.clip(jax.random.uniform(streams_of[7], (MM,), jnp.float32, -1.0, 1.0), -1.0, 1.0)
    return dict(composition=composition, cotangent=cotangent, weight_one=weight_one, bias_one=bias_one, weight_two=weight_two, bias_two=bias_two, weight_three=weight_three, bias_three=bias_three)


step_size = 0.08
cubic_coef = 0.1
diag_scale = 0.5
off_scale = 0.04

def potential(values):
    return values + cubic_coef * values * values * values

def potential_slope(values):
    return 1.0 + 3.0 * cubic_coef * values * values

def mobility_tables(channels):
    position = jnp.arange(channels * channels, dtype=jnp.int32)
    on_diagonal = position // channels == position % channels
    identity = jnp.where(on_diagonal, 1.0, 0.0).astype(jnp.float32)
    scales = jnp.where(on_diagonal, diag_scale, off_scale).astype(jnp.float32)
    return (identity, scales)

def forward_net(flattened, weights):
    weight_one, bias_one, weight_two, bias_two, weight_three, bias_three = weights
    identity, scales = mobility_tables(flattened.shape[0])
    inputs = flattened.astype(jnp.bfloat16)
    hidden_one = jnp.tanh(jnp.dot(weight_one, inputs, preferred_element_type=jnp.float32) + bias_one[:, None]).astype(jnp.bfloat16)
    hidden_two = jnp.tanh(jnp.dot(weight_two, hidden_one, preferred_element_type=jnp.float32) + bias_two[:, None]).astype(jnp.bfloat16)
    active = jnp.tanh(jnp.dot(weight_three, hidden_two, preferred_element_type=jnp.float32) + bias_three[:, None])
    mobility = identity[:, None] + scales[:, None] * active
    return (mobility, (inputs, hidden_one, hidden_two, active))

def backward_net(grad_mob, stored, weights):
    weight_one, bias_one, weight_two, bias_two, weight_three, bias_three = weights
    inputs, hidden_one, hidden_two, active = stored
    _, scales = mobility_tables(inputs.shape[0])
    pre_three = (grad_mob * scales[:, None] * (1.0 - active * active)).astype(jnp.bfloat16)
    upper_two = hidden_two.astype(jnp.float32)
    pre_two = (jnp.dot(weight_three.T, pre_three, preferred_element_type=jnp.float32) * (1.0 - upper_two * upper_two)).astype(jnp.bfloat16)
    upper_one = hidden_one.astype(jnp.float32)
    pre_one = (jnp.dot(weight_two.T, pre_two, preferred_element_type=jnp.float32) * (1.0 - upper_one * upper_one)).astype(jnp.bfloat16)
    net_grad = jnp.dot(weight_one.T, pre_one, preferred_element_type=jnp.float32)
    grads = (jnp.dot(pre_one, inputs.T, preferred_element_type=jnp.float32), lax.optimization_barrier(jnp.sum(pre_one.astype(jnp.float32), axis=1)), jnp.dot(pre_two, hidden_one.T, preferred_element_type=jnp.float32), lax.optimization_barrier(jnp.sum(pre_two.astype(jnp.float32), axis=1)), jnp.dot(pre_three, hidden_two.T, preferred_element_type=jnp.float32), lax.optimization_barrier(jnp.sum(pre_three.astype(jnp.float32), axis=1)))
    return (net_grad, grads)

def apply_mobility(mobility, vector):
    channels = vector.shape[0]
    matrix = mobility.reshape((channels, channels) + vector.shape[1:])
    return lax.optimization_barrier(jnp.sum(matrix * vector[None], axis=1))

def apply_transpose(mobility, vector):
    channels = vector.shape[0]
    matrix = mobility.reshape((channels, channels) + vector.shape[1:])
    return lax.optimization_barrier(jnp.sum(matrix * vector[:, None], axis=0))

def outer_terms(adjoint, pot_jump):
    channels = adjoint.shape[0]
    return (adjoint[:, None] * pot_jump[None]).reshape((channels * channels,) + adjoint.shape[1:])

def plane_at(array, position):
    return lax.dynamic_index_in_dim(array, position, 1, keepdims=False)

def plane_network(plane, weights):
    channels = plane.shape[0]
    mobility, stored = forward_net(plane.reshape(channels, -1), weights)
    return (mobility.reshape((channels * channels,) + plane.shape[1:]), stored)

def forward_step(current, weights):
    plane_count = current.shape[1]
    potentials = potential(current)
    first_mob, _ = plane_network(current[:, plane_count - 1], weights)
    second_mob, _ = plane_network(current[:, 0], weights)

    def advance(state_carry, position):
        lower_mob, middle_mob = state_carry
        upper_index = (position + 1) % plane_count
        lower_index = (position + plane_count - 1) % plane_count
        upper_mob, _ = plane_network(plane_at(current, upper_index), weights)
        pot_low = plane_at(potentials, lower_index)
        pot_mid = plane_at(potentials, position)
        pot_high = plane_at(potentials, upper_index)
        flux_up = apply_mobility(0.5 * (middle_mob + upper_mob), pot_high - pot_mid)
        flux_down = apply_mobility(0.5 * (lower_mob + middle_mob), pot_mid - pot_low)
        change = flux_up - flux_down
        for spatial in (1, 2):
            shifted_mob = jnp.roll(middle_mob, -1, axis=spatial)
            face_flux = apply_mobility(0.5 * (middle_mob + shifted_mob), jnp.roll(pot_mid, -1, axis=spatial) - pot_mid)
            change = change + (face_flux - jnp.roll(face_flux, 1, axis=spatial))
        return ((middle_mob, upper_mob), plane_at(current, position) + step_size * change)
    _, planes = lax.scan(advance, (first_mob, second_mob), jnp.arange(plane_count, dtype=jnp.int32))
    return jnp.moveaxis(planes, 0, 1)

def backward_step(current, incoming, weights):
    plane_count = current.shape[1]
    potentials = potential(current)
    first_mob, _ = plane_network(current[:, plane_count - 1], weights)
    second_mob, second_stored = plane_network(current[:, 0], weights)
    zero_grads = tuple((jnp.zeros(member.shape, jnp.float32) for member in weights))

    def retreat(state_carry, position):
        lower_mob, middle_mob, middle_stored, totals = state_carry
        upper_index = (position + 1) % plane_count
        lower_index = (position + plane_count - 1) % plane_count
        upper_mob, upper_stored = plane_network(plane_at(current, upper_index), weights)
        pot_low = plane_at(potentials, lower_index)
        pot_mid = plane_at(potentials, position)
        pot_high = plane_at(potentials, upper_index)
        adj_low = plane_at(incoming, lower_index)
        adj_mid = plane_at(incoming, position)
        adj_high = plane_at(incoming, upper_index)
        adjoint_up = step_size * (adj_mid - adj_high)
        adjoint_down = step_size * (adj_low - adj_mid)
        mob_up = 0.5 * (middle_mob + upper_mob)
        mob_down = 0.5 * (lower_mob + middle_mob)
        grad_pot = apply_transpose(mob_down, adjoint_down) - apply_transpose(mob_up, adjoint_up)
        grad_mob = outer_terms(adjoint_down, pot_mid - pot_low) + outer_terms(adjoint_up, pot_high - pot_mid)
        for spatial in (1, 2):
            shifted_mob = jnp.roll(middle_mob, -1, axis=spatial)
            pot_jump = jnp.roll(pot_mid, -1, axis=spatial) - pot_mid
            adjoint = step_size * (adj_mid - jnp.roll(adj_mid, -1, axis=spatial))
            back_flow = apply_transpose(0.5 * (middle_mob + shifted_mob), adjoint)
            grad_pot = grad_pot + (jnp.roll(back_flow, 1, axis=spatial) - back_flow)
            outer_prod = outer_terms(adjoint, pot_jump)
            grad_mob = grad_mob + (jnp.roll(outer_prod, 1, axis=spatial) + outer_prod)
        grad_mob = 0.5 * grad_mob
        net_grad, grads = backward_net(grad_mob.reshape(grad_mob.shape[0], -1), middle_stored, weights)
        plane_state = plane_at(current, position)
        outgoing = adj_mid + grad_pot * potential_slope(plane_state) + net_grad.reshape(plane_state.shape)
        totals = tuple((running + current_grad for running, current_grad in zip(totals, grads)))
        return ((middle_mob, upper_mob, upper_stored, totals), outgoing)
    final_carry, planes = lax.scan(retreat, (first_mob, second_mob, second_stored, zero_grads), jnp.arange(plane_count, dtype=jnp.int32))
    return (jnp.moveaxis(planes, 0, 1), final_carry[3])

def reference(composition, cotangent, weight_one, bias_one, weight_two, bias_two, weight_three, bias_three):
    weights = (weight_one, bias_one, weight_two, bias_two, weight_three, bias_three)
    state_one = forward_step(composition, weights)
    cotangent_one, late_grads = backward_step(state_one, cotangent, weights)
    grad_composition, early_grads = backward_step(composition, cotangent_one, weights)
    factor = 1.0 / (step_size * math.sqrt(NX * NY * NZ))
    scaled = tuple(((late + early) * factor for late, early in zip(late_grads, early_grads)))
    return (grad_composition, scaled[0], scaled[1], scaled[2], scaled[3], scaled[4], scaled[5])
```

```python
import functools
import math

import jax
import jax.numpy as jnp
from jax import lax
from jax.experimental import pallas as pl
from jax.experimental.pallas import tpu as pltpu
from jax.sharding import PartitionSpec as P

step_size = 0.08
cubic_coef = 0.1
diag_scale = 0.5
off_scale = 0.04
axes = ("gx", "gy", "gz")
F32 = jnp.float32
BF16 = jnp.bfloat16


def potential(v):
    return v + cubic_coef * v * v * v


def iota(shape, dim):
    return lax.broadcasted_iota(jnp.int32, shape, dim)


def dot(a, b):
    return jnp.dot(a, b, preferred_element_type=F32)


def dot_nt(a, b):
    return lax.dot_general(a, b, (((1,), (1,)), ((), ())), preferred_element_type=F32)


def split_two(v):
    high = v.astype(BF16)
    return high, (v - high.astype(F32)).astype(BF16)


def rolled(v, shift, axis):
    shift = shift % v.shape[axis]
    return pltpu.roll(v, shift, axis) if shift else v


def log2(n):
    assert n & (n - 1) == 0
    return n.bit_length() - 1


def kernel(
    dims, comp, cot, w1, b1, w2, b2, w3, b3, out, pay,
    vec, ybuf, zbuf, xhalo, yhalo, zhalo,
    w1x, w1t, w2x, w2t, w3x, w3t, e3, bb1, bb2, bb3,
    xin, hid1, hid2, act, arim, dpot, dcot, drim, tin, trim, pack, p3, r1, r2, r3, q1, q2, q3,
    send_sem, recv_sem,
):
    nc, nx, ny, nz, h1, h2 = dims
    width = nx * nz
    mm = nc * nc
    sy = log2(ny)
    grp = 256 // h1

    here = {a: lax.axis_index(a) for a in axes}
    size = {a: lax.axis_size(a) for a in axes}
    up = {a: {a: lax.rem(here[a] + 1, size[a])} for a in axes}
    down = {a: {a: lax.rem(here[a] + size[a] - 1, size[a])} for a in axes}
    barrier = pltpu.get_barrier_semaphore()
    for a in axes:
        for target in (up[a], down[a]):
            pl.semaphore_signal(barrier, inc=1, device_id=target, device_id_type=pl.DeviceIdType.MESH)

    lane3 = iota((nc, ny, nz), 2)
    row3 = iota((nc, ny, nz), 1)
    lane2 = iota((ny, nz), 1)

    def planes(v):
        return [v[:, :, x * nz : (x + 1) * nz] for x in range(nx)]

    def own_ends(v):
        total = jnp.zeros((nc, ny, nz), F32)
        for x, plane in enumerate(planes(v)):
            total = jnp.where(lane3 == x, rolled(plane, x, 2), total)
            total = jnp.where(lane3 == nx + x, rolled(plane, nx + x + 1, 2), total)
        return total

    def fill(e):
        for c in range(nc):
            for x in range(nx):
                cols = slice(x * nz, (x + 1) * nz)
                ybuf[e, 0, c * nx + x : c * nx + x + 1, :] = vec[e, c, 0:1, cols]
                ybuf[e, 1, c * nx + x : c * nx + x + 1, :] = vec[e, c, ny - 1 : ny, cols]
        ends = own_ends(vec[e])
        total = ends[0]
        for c in range(1, nc):
            total = total + rolled(ends[c], c * 2 * nx, 1)
        zbuf[e] = total

    def copies(e):
        moves = (
            (vec.at[e, :, :, width - nz : width], xhalo.at[e, 0], up["gx"]),
            (vec.at[e, :, :, 0:nz], xhalo.at[e, 1], down["gx"]),
            (ybuf.at[e, 1], yhalo.at[e, 0], up["gy"]),
            (ybuf.at[e, 0], yhalo.at[e, 1], down["gy"]),
            (zbuf.at[e], zhalo.at[e, 0], up["gz"]),
            (zbuf.at[e], zhalo.at[e, 1], down["gz"]),
        )
        return [
            pltpu.make_async_remote_copy(
                src_ref=src, dst_ref=dst, send_sem=send_sem.at[e, k], recv_sem=recv_sem.at[e, k],
                device_id=target, device_id_type=pl.DeviceIdType.MESH,
            )
            for k, (src, dst, target) in enumerate(moves)
        ]

    def start(e):
        for copy in copies(e):
            copy.start()

    def finish(e):
        for copy in copies(e):
            copy.wait()

    def received_ends(e):
        phase = lane2 & (2 * nx - 1)
        low = jnp.where(phase < nx, rolled(zhalo[e, 0], -nx, 1), 0.0)
        high = jnp.where(phase >= nx, rolled(zhalo[e, 1], nx, 1), 0.0)
        total = low + high
        return jnp.stack([rolled(total, -c * 2 * nx, 1) for c in range(nc)], axis=0)

    def packed(low, high, ends):
        for c in range(nc):
            pack[c, 0:nx, :] = low[c * nx : (c + 1) * nx, :]
            pack[c, nx : 2 * nx, :] = high[c * nx : (c + 1) * nx, :]
        half = ny // 2
        folded = jnp.where(lane3 < 2 * nx, rolled(ends, half, 1), rolled(ends, 2 * nx, 2))
        folded = jnp.where(lane3 < 4 * nx, folded, 0.0)
        return jnp.where(row3 < half, pack[...], folded)

    def neighbours(v, low_x, high_x, rim, ends):
        parts = planes(v)
        x_low = jnp.concatenate([low_x] + parts[:-1], axis=2)
        x_high = jnp.concatenate(parts[1:] + [high_x], axis=2)
        found = [[], [], [], []]
        for x, plane in enumerate(parts):
            found[0].append(jnp.where(row3 == 0, rim[:, x : x + 1, :], rolled(plane, 1, 1)))
            found[1].append(
                jnp.where(row3 == ny - 1, rim[:, nx + x : nx + x + 1, :], rolled(plane, -1, 1))
            )
            found[2].append(jnp.where(lane3 == 0, rolled(ends, -x, 2), rolled(plane, 1, 2)))
            found[3].append(
                jnp.where(lane3 == nz - 1, rolled(ends, nz - 1 - nx - x, 2), rolled(plane, -1, 2))
            )
        return [x_low, x_high] + [jnp.concatenate(f, axis=2) for f in found]

    def halo(e):
        ends = received_ends(e)
        rim = packed(yhalo[e, 0], yhalo[e, 1], ends)
        return xhalo[e, 0], xhalo[e, 1], rim, ends

    def differences(e, inner, low_x, high_x, rim, ends, mapping, target, which):
        v = mapping(inner)
        lx, hx, mrim = mapping(low_x), mapping(high_x), mapping(rim)
        for d, other in enumerate(neighbours(v, lx, hx, mrim, mapping(ends))):
            target[d] = v - other
        own = mapping(packed(ybuf[e, 0], ybuf[e, 1], own_ends(inner)))
        drim[which] = jnp.concatenate(
            [lx - v[:, :, 0:nz], hx - v[:, :, width - nz : width], mrim - own], axis=2
        )

    def net(v, target, keep):
        lanes = v.shape[2]

        def wide(ref):
            return jnp.concatenate([ref[...]] * (lanes // 128), axis=1)

        flat = v.reshape(nc * ny, lanes).astype(BF16)
        one = jnp.tanh(dot(w1x[...], flat) + wide(bb1)).astype(BF16)
        bias = wide(bb2)
        two = []
        span = grp * h1
        for g in range(ny // grp):
            rows = slice(g * span, (g + 1) * span)
            two.append(jnp.tanh(dot(w2x[...], one[rows]) + bias[rows]).astype(BF16))
        two = jnp.concatenate(two, axis=0)
        target[...] = jnp.tanh(dot(w3x[...], two) + wide(bb3))
        if keep is not None:
            xin[keep] = flat
            hid1[keep] = one
            hid2[keep] = two

    def apply(a_ref, d_ref, t_ref, count, transposed):
        def body(k, carry):
            sums = [None] * count
            for q in range(nc):
                at = (q * nc + k) * ny if transposed else (k * nc + q) * ny
                m = a_ref[pl.ds(pl.multiple_of(at, ny), ny), :]
                for d in range(count):
                    term = m * d_ref[d, q]
                    sums[d] = term if sums[d] is None else sums[d] + term
            at = pl.multiple_of(k * (nc + 1) * ny, ny)
            own = 1.0 + (diag_scale - off_scale) * a_ref[pl.ds(at, ny), :]
            for d in range(count):
                t_ref[d, k] = d_ref[d, k] * own + off_scale * sums[d]
            return carry

        lax.fori_loop(0, nc, body, 0)

    def inner_flow(s, d_ref, transposed):
        apply(act.at[s], d_ref, tin, 6, transposed)
        total = -(tin[0] + tin[1] + tin[2] + tin[3] + tin[4] + tin[5])
        zero = jnp.zeros((nc, ny, nz), F32)
        low, high = planes(tin[0]), planes(tin[1])
        total = total + jnp.concatenate(low[1:] + [zero], axis=2)
        total = total + jnp.concatenate([zero] + high[:-1], axis=2)
        moved = []
        for x in range(nx):
            cols = slice(x * nz, (x + 1) * nz)
            to_low_y = jnp.where(row3 == ny - 1, 0.0, rolled(tin[2, :, :, cols], -1, 1))
            to_high_y = jnp.where(row3 == 0, 0.0, rolled(tin[3, :, :, cols], 1, 1))
            to_low_z = jnp.where(lane3 == nz - 1, 0.0, rolled(tin[4, :, :, cols], -1, 2))
            to_high_z = jnp.where(lane3 == 0, 0.0, rolled(tin[5, :, :, cols], 1, 2))
            moved.append((to_low_y + to_high_y) + (to_low_z + to_high_z))
        return total + jnp.concatenate(moved, axis=2)

    def rim_flow(s, which, transposed):
        apply(arim.at[s], drim.at[pl.ds(which, 1)], trim, 1, transposed)
        half = ny // 2
        t = trim[0, :, :, 2 * nz : 3 * nz]
        ends = jnp.where(row3 < half, rolled(t, half, 1), rolled(t, -2 * nx, 2))
        parts = []
        for x in range(nx):
            part = jnp.where(row3 == 0, t[:, x : x + 1, :], 0.0)
            part = part + jnp.where(row3 == ny - 1, t[:, nx + x : nx + x + 1, :], 0.0)
            part = part + jnp.where(lane3 == 0, rolled(ends, -x, 2), 0.0)
            part = part + jnp.where(lane3 == nz - 1, rolled(ends, nz - 1 - nx - x, 2), 0.0)
            if x == 0:
                part = part + trim[0, :, :, 0:nz]
            if x == nx - 1:
                part = part + trim[0, :, :, nz : 2 * nz]
            parts.append(part)
        return jnp.concatenate(parts, axis=2)

    def back_net(s, first):
        def body(a, carry):
            left = [dcot[d, a] for d in range(6)]
            for b in range(0, nc, 2):
                pair = []
                for k in (b, b + 1):
                    total = left[0] * dpot[s, 0, k]
                    for d in range(1, 6):
                        total = total + left[d] * dpot[s, d, k]
                    at = pl.multiple_of((a * nc + k) * ny, ny)
                    active = act[s, pl.ds(at, ny), :]
                    scale = jnp.where(a == k, -0.5 * step_size * diag_scale, -0.5 * step_size * off_scale)
                    pair.append(total * scale * (1.0 - active * active))
                at = pl.multiple_of((a * nc + b) * ny, 2 * ny)
                p3[pl.ds(at, 2 * ny), :] = jnp.concatenate(pair, axis=0).astype(BF16)
            return carry

        lax.fori_loop(0, nc, body, 0)
        pre_three = p3[...]
        two = hid2[s]
        one = hid1[s]
        upper = two.astype(F32)
        pre_two = (dot(w3t[...], pre_three) * (1.0 - upper * upper)).astype(BF16)
        upper = one.astype(F32)
        span = grp * h1
        pre_one = []
        for g in range(ny // grp):
            rows = slice(g * span, (g + 1) * span)
            pre_one.append(
                (dot(w2t[...], pre_two[rows]) * (1.0 - upper[rows] * upper[rows])).astype(BF16)
            )
        pre_one = jnp.concatenate(pre_one, axis=0)
        net_grad = dot(w1t[...], pre_one).reshape(nc, ny, width)

        def grads():
            even = odd = None
            for y in range(0, ny, 2):
                pair = one[y * h1 : (y + 2) * h1]
                e_term = dot_nt(pre_two[y * h2 : (y + 1) * h2], pair)
                o_term = dot_nt(pre_two[(y + 1) * h2 : (y + 2) * h2], pair)
                even = e_term if even is None else even + e_term
                odd = o_term if odd is None else odd + o_term

            def over_rows(v, rows):
                v = v.astype(F32)
                total = v[0:rows]
                for y in range(1, ny):
                    total = total + v[y * rows : (y + 1) * rows]
                return total

            values = (
                (r1, dot_nt(pre_one, xin[s])),
                (r2, odd + rolled(even, h1, 1)),
                (r3, dot_nt(pre_three, two)),
                (q1, over_rows(pre_one, h1)),
                (q2, over_rows(pre_two, h2)),
                (q3, dot(e3[...], pre_three)),
            )
            for ref, value in values:
                ref[...] = value if first else ref[...] + value

        return net_grad, grads

    for x in range(nx):
        vec[0, :, :, x * nz : (x + 1) * nz] = comp[:, x]
        vec[1, :, :, x * nz : (x + 1) * nz] = cot[:, x]
    fill(0)
    fill(1)
    pl.semaphore_wait(barrier, 6)
    start(0)
    start(1)

    sh = log2(h1)
    rows_h, rows_m, rows_c = ny * h1, mm * ny, nc * ny

    def select(mask, value):
        return jnp.where(mask, value, 0.0).astype(BF16)

    def ones(mask):
        return jnp.where(mask, 1.0, 0.0).astype(BF16)

    tile = ones((iota((h1, rows_h), 1) & (h1 - 1)) == iota((h1, rows_h), 0))
    unit = ones(iota((h1, h1), 1) == iota((h1, h1), 0))
    spread_c = ones((iota((nc, rows_c), 1) >> sy) == iota((nc, rows_c), 0))
    spread_ct = ones((iota((rows_c, nc), 0) >> sy) == iota((rows_c, nc), 1))
    spread_mt = ones((iota((rows_m, mm), 0) >> sy) == iota((rows_m, mm), 1))
    e3[...] = ones((iota((mm, rows_m), 1) >> sy) == iota((mm, rows_m), 0))

    mask_hc = (iota((rows_h, rows_c), 0) >> sh) == (iota((rows_h, rows_c), 1) & (ny - 1))
    w1x[...] = select(mask_hc, jnp.concatenate([dot(w1[...], spread_c)] * ny, axis=0))
    mask_ch = (iota((rows_c, rows_h), 1) >> sh) == (iota((rows_c, rows_h), 0) & (ny - 1))
    w1t[...] = select(mask_ch, dot(dot_nt(spread_ct, w1[...]).astype(BF16), tile))
    span = grp * h1
    mask_g = (iota((span, span), 0) >> sh) == (iota((span, span), 1) >> sh)
    flipped = dot_nt(unit, w2[...]).astype(BF16)
    w2x[...] = select(mask_g, jnp.concatenate([dot(w2[...], tile[:, 0:span])] * grp, axis=0))
    w2t[...] = select(mask_g, jnp.concatenate([dot(flipped, tile[:, 0:span])] * grp, axis=0))
    mask_mh = (iota((rows_m, rows_h), 0) & (ny - 1)) == (iota((rows_m, rows_h), 1) >> sh)
    w3x[...] = select(mask_mh, dot(dot(spread_mt, w3[...]).astype(BF16), tile))
    mask_hm = (iota((rows_h, rows_m), 1) & (ny - 1)) == (iota((rows_h, rows_m), 0) >> sh)
    flipped = dot_nt(unit, w3[...]).astype(BF16)
    w3t[...] = select(mask_hm, jnp.concatenate([dot(flipped, e3[...])] * ny, axis=0))

    def column(mask, b):
        return jnp.sum(jnp.where(mask, b[...], 0.0), axis=1, keepdims=True)

    mask_b = (iota((rows_h, h1), 0) & (h1 - 1)) == iota((rows_h, h1), 1)
    bb1[...] = jnp.broadcast_to(column(mask_b, b1), bb1.shape)
    bb2[...] = jnp.broadcast_to(column(mask_b, b2), bb2.shape)
    mask_b = (iota((rows_m, mm), 0) >> sy) == iota((rows_m, mm), 1)
    bb3[...] = jnp.broadcast_to(column(mask_b, b3), bb3.shape)

    def same(v):
        return v

    net(vec[0], act.at[0], 0)
    finish(0)
    low_x, high_x, rim, ends = halo(0)
    net(jnp.concatenate([low_x, high_x, rim], axis=2), arim.at[0], None)
    differences(0, vec[0], low_x, high_x, rim, ends, potential, dpot.at[0], 0)
    vec[2] = vec[0] + 0.5 * step_size * (inner_flow(0, dpot.at[0], False) + rim_flow(0, 0, False))
    fill(2)
    start(2)

    net(vec[2], act.at[1], 1)
    finish(1)
    low_x, high_x, rim, ends = halo(1)
    differences(1, vec[1], low_x, high_x, rim, ends, same, dcot, 0)
    flow = inner_flow(1, dcot, True)
    finish(2)
    low_x, high_x, rim, ends = halo(2)
    net(jnp.concatenate([low_x, high_x, rim], axis=2), arim.at[1], None)
    differences(2, vec[2], low_x, high_x, rim, ends, potential, dpot.at[1], 1)
    flow = flow + rim_flow(1, 0, True)
    net_grad, grads = back_net(1, True)

    def slope(v):
        return 1.0 + 3.0 * cubic_coef * v * v

    vec[3] = vec[1] + 0.5 * step_size * flow * slope(vec[2]) + net_grad
    fill(3)
    start(3)
    grads()

    finish(3)
    low_x, high_x, rim, ends = halo(3)
    differences(3, vec[3], low_x, high_x, rim, ends, same, dcot, 0)
    net_grad, grads = back_net(0, False)
    grads()
    flow = inner_flow(0, dcot, True) + rim_flow(0, 0, True)
    result = vec[3] + 0.5 * step_size * flow * slope(vec[0]) + net_grad
    for x in range(nx):
        out[:, x] = result[:, :, x * nz : (x + 1) * nz]

    high, low = split_two(jnp.where(mask_mh, r3[...], 0.0))
    wide = dot(e3[...], high) + dot(e3[...], low)
    fold = wide[:, 0:128]
    for k in range(1, rows_h // 128):
        fold = fold + wide[:, k * 128 : (k + 1) * 128]
    fold = fold + rolled(fold, h1, 1)
    first = jnp.where(mask_hc, r1[...], 0.0)
    total = first[0:h1]
    for y in range(1, ny):
        total = total + first[y * h1 : (y + 1) * h1]
    place = ones(iota((rows_c, 128), 1) == h1 + (iota((rows_c, 128), 0) >> sy))
    high, low = split_two(total)
    one = dot(high, place) + dot(low, place)
    s1 = jnp.sum(q1[...], axis=1, keepdims=True)
    s2 = jnp.sum(q2[...], axis=1, keepdims=True)
    s3 = jnp.sum(q3[...], axis=1, keepdims=True)
    lane = iota((h1, 128), 1)
    at = h1 + nc
    for k, part in enumerate((s1, s2, s3[0:h1], s3[h1 : 2 * h1])):
        one = jnp.where(lane == at + k, part, one)
    pay[0:h1, :] = jnp.where(lane < h1, fold[0:h1], r2[...])
    pay[h1 : 2 * h1, :] = jnp.where(lane < h1, fold[h1 : 2 * h1], one)
    rest = mm - 2 * h1
    pay[2 * h1 : mm, :] = jnp.where(
        iota((rest, 128), 1) < h1, fold[2 * h1 : mm], s3[2 * h1 : mm]
    )


def shards(
    composition, cotangent, weight_one, bias_one, weight_two, bias_two, weight_three, bias_three
):
    nc, nx, ny, nz = composition.shape
    h1, h2 = weight_one.shape[0], weight_two.shape[0]
    mm = nc * nc
    width = nx * nz
    assert h1 == h2 and 2 * h1 == 128 and nz == 128 and 4 * nx == ny and 2 * h1 <= mm
    rows_h, rows_m, rows_c = ny * h1, mm * ny, nc * ny
    span = 256 // h1 * h1
    vmem = pltpu.VMEM
    result, pay = pl.pallas_call(
        functools.partial(kernel, (nc, nx, ny, nz, h1, h2)),
        out_shape=(
            jax.ShapeDtypeStruct(composition.shape, F32),
            jax.ShapeDtypeStruct((mm, 128), F32),
        ),
        in_specs=[pl.BlockSpec(memory_space=vmem)] * 8,
        out_specs=(pl.BlockSpec(memory_space=vmem), pl.BlockSpec(memory_space=vmem)),
        scratch_shapes=[
            vmem((4, nc, ny, width), F32),
            vmem((4, 2, nc * nx, nz), F32),
            vmem((4, ny, nz), F32),
            vmem((4, 2, nc, ny, nz), F32),
            vmem((4, 2, nc * nx, nz), F32),
            vmem((4, 2, ny, nz), F32),
            vmem((rows_h, rows_c), BF16),
            vmem((rows_c, rows_h), BF16),
            vmem((span, span), BF16),
            vmem((span, span), BF16),
            vmem((rows_m, rows_h), BF16),
            vmem((rows_h, rows_m), BF16),
            vmem((mm, rows_m), BF16),
            vmem((rows_h, 128), F32),
            vmem((rows_h, 128), F32),
            vmem((rows_m, 128), F32),
            vmem((2, rows_c, width), BF16),
            vmem((2, rows_h, width), BF16),
            vmem((2, rows_h, width), BF16),
            vmem((2, rows_m, width), F32),
            vmem((2, rows_m, 3 * nz), F32),
            vmem((2, 6, nc, ny, width), F32),
            vmem((6, nc, ny, width), F32),
            vmem((2, nc, ny, 3 * nz), F32),
            vmem((6, nc, ny, width), F32),
            vmem((1, nc, ny, 3 * nz), F32),
            vmem((nc, ny, nz), F32),
            vmem((rows_m, width), BF16),
            vmem((rows_h, rows_c), F32),
            vmem((h2, 2 * h1), F32),
            vmem((rows_m, rows_h), F32),
            vmem((h1, width), F32),
            vmem((h2, width), F32),
            vmem((mm, width), F32),
            pltpu.SemaphoreType.DMA((4, 6)),
            pltpu.SemaphoreType.DMA((4, 6)),
        ],
        compiler_params=pltpu.CompilerParams(
            collective_id=0, has_side_effects=True, vmem_limit_bytes=56 * 1024 * 1024
        ),
    )(
        composition,
        cotangent,
        weight_one,
        bias_one.reshape(1, h1),
        weight_two,
        bias_two.reshape(1, h2),
        weight_three,
        bias_three.reshape(1, mm),
    )
    cells = nx * ny * nz
    for a in axes:
        cells = cells * lax.axis_size(a)
    pay = lax.psum(pay, axes) * (1.0 / (step_size * math.sqrt(cells)))
    at = h1 + nc
    return (
        result,
        pay[h1 : 2 * h1, h1 : h1 + nc],
        pay[h1 : 2 * h1, at],
        pay[0:h1, h1:],
        pay[h1 : 2 * h1, at + 1],
        pay[:, 0:h1],
        jnp.concatenate(
            [pay[h1 : 2 * h1, at + 2], pay[h1 : 2 * h1, at + 3], pay[2 * h1 : mm, h1]]
        ),
    )


def solution(mesh):
    in_specs = (P(None, "gx", "gy", "gz"), P(None, "gx", "gy", "gz"), P(), P(), P(), P(), P(), P())
    out_specs = (P(None, "gx", "gy", "gz"), P(), P(), P(), P(), P(), P())
    return jax.shard_map(shards, mesh=mesh, in_specs=in_specs, out_specs=out_specs, check_vma=False)
```
